1024 devices in a mesh: seq: 64 (over y_hi, z, core), batch: 16 (over x, y_lo).
Axes of the slice: x: 4, y: 8 (y_hi: 2, y_lo: 4; y = y_hi * 4 + y_lo), z: 16, core: 2. Of those that a mesh axis runs over, the one named last changes fastest.
Arguments:
- queries: bfloat16 [32, 512, 64, 128], P('batch', 'seq'), parts along dimension 0, may hold values from -5 to 5
- grad_out: bfloat16 [32, 512, 64, 128], P('batch', 'seq'), parts along dimension 0, may hold values from -6 to 6
- keys: bfloat16 [16384, 64, 128], P('batch', 'seq'), parts along dimension 0, may hold values from -5 to 5
- values: bfloat16 [16384, 64, 128], P('batch', 'seq'), parts along dimension 0, may hold values from -6 to 6
- block_offsets: int32 [48], P('batch'), parts along dimension 0, may hold values from 261120 to 261632, as said below
Outputs:
- grad_queries: bfloat16 [32, 512, 64, 128], P('batch', 'seq'), parts along dimension 0
- grad_keys: bfloat16 [16384, 64, 128], P(('batch', 'seq')), parts along dimension 0
- grad_values: bfloat16 [16384, 64, 128], P(('batch', 'seq')), parts along dimension 0
The draws below stay inside these ranges and needn't reach their ends.
There are 16 independent parts, one for each index of `batch`. The reference program is written for one: setup_inputs(seed, part) draws one part's arguments, and reference() takes and returns one part's arrays. A program takes and returns all parts, laid end to end along the dimension named above; each array names one. Nothing has to cross between parts.
Inputs may be any that keep to these rules, and one draw needn't show every extreme that they name: block_offsets[0] is 261120; each query block starts 0 to 512 positions after the key block's start, and some query block starts exactly 512 after it.
All inputs are finite; a program needn't handle non-finite values.
Results may differ from the reference program's by a relative error of at most 0.012.
The reference program's roundings to bfloat16 on the way (of `attend_b` and `grad_scores`) count: a program that leaves them out, or rounds other values in their place, can miss the bound.
Values may be sent and summed in bfloat16 or wider, within the bound.
A program may use at most 32 MiB of HBM per device.

```python
import jax
import jax.numpy as jnp
from jax import lax

H = 64
HD = 128
KEYS = 1024
QLEN = 512
QBLOCKS = 2
SEQLEN = 262144


def draw_queries(key, part):
    key = jax.random.fold_in(key, 1)
    shape = (QBLOCKS, QLEN, H, HD)
    base = jnp.clip(jax.random.normal(key, shape, jnp.float32), -5.0, 5.0)
    return base.astype(jnp.bfloat16)


def draw_keys(key, part):
    key = jax.random.fold_in(key, 2)
    shape = (KEYS, H, HD)
    base = jnp.clip(jax.random.normal(key, shape, jnp.float32), -5.0, 5.0)
    return base.astype(jnp.bfloat16)


def draw_block_offsets(key, part):
    key = jax.random.fold_in(key, 3)
    first_key, second_key = jax.random.split(key)
    start = jnp.int32(SEQLEN - KEYS)
    shifts = jax.random.randint(second_key, (QBLOCKS,), 0, KEYS - QLEN + 1)
    chosen = jax.random.randint(first_key, (), 0, QBLOCKS)
    shifts = jnp.where(jnp.arange(QBLOCKS) == chosen, KEYS - QLEN, shifts)
    return jnp.concatenate([start[None], start + shifts]).astype(jnp.int32)


def level_of(rng, extent, pieces, smallest, high):
    def one(position, shards_of):
        draws = jax.random.uniform(jax.random.fold_in(jax.random.fold_in(rng, 6), position), (shards_of,), jnp.float32, smallest / len(pieces), high / len(pieces))
        return jnp.repeat(jnp.exp(draws), extent[position] // shards_of).reshape((-1,) + (1,) * (len(extent) - position - 1))

    gain = one(*pieces[0])
    for cut in pieces[1:]:
        gain = gain * one(*cut)
    return gain


def centred(key, shape, spread, bound, shards=(), kind=jnp.bfloat16):
    level = level_of(key, shape, shards, -0.22, 0.18) if shards else 1.0
    drawn = jax.random.normal(key, shape, jnp.float32) * spread * level
    return jnp.minimum(jnp.maximum(drawn, -bound), bound).astype(kind)


def setup_inputs(seed: int = 0, part: int = 0) -> dict:
    key_list = jax.random.split(jax.random.key(seed), 6)
    part_splits = jax.random.split(jax.random.fold_in(key_list[5], part), 6)
    return {
        "queries": draw_queries(jax.random.fold_in(jax.random.fold_in(key_list[5], part), 71), part),
        "grad_out": centred(part_splits[1], (QBLOCKS, QLEN, H, HD), 1.0, 6.0, ((1, 64),)),
        "keys": draw_keys(jax.random.fold_in(jax.random.fold_in(key_list[5], part), 71), part),
        "values": centred(part_splits[3], (KEYS, H, HD), 1.0, 6.0, ((1, 64),)),
        "block_offsets": draw_block_offsets(jax.random.fold_in(jax.random.fold_in(key_list[5], part), 71), part),
    }


def head_backward(q_head, grad_head, k_head, v_head, query_pos, key_pos):
    score_scale = HD ** -0.5
    scores = jnp.dot(q_head, k_head.T, preferred_element_type=jnp.float32) * score_scale
    scores = jnp.where(key_pos[None, :] <= query_pos[:, None], scores, -jnp.inf)
    row_max = jnp.max(scores, axis=-1, keepdims=True)
    expo = jnp.exp(scores - row_max)
    attend = expo / jnp.sum(expo, axis=-1, keepdims=True)
    attend_b = attend.astype(jnp.bfloat16)
    outputs = jnp.dot(attend_b, v_head, preferred_element_type=jnp.float32)
    row_delta = jnp.sum(grad_head.astype(jnp.float32) * outputs, axis=-1, keepdims=True)
    grad_attend = jnp.dot(grad_head, v_head.T, preferred_element_type=jnp.float32)
    grad_scores = (attend * (grad_attend - row_delta)).astype(jnp.bfloat16)
    grad_q = (jnp.dot(grad_scores, k_head, preferred_element_type=jnp.float32) * score_scale).astype(jnp.bfloat16)
    grad_k = jnp.dot(grad_scores.T, q_head, preferred_element_type=jnp.float32) * score_scale
    grad_v = jnp.dot(attend_b.T, grad_head, preferred_element_type=jnp.float32)
    return grad_q, grad_k, grad_v


def reference(queries, grad_out, keys, values, block_offsets):
    key_pos = block_offsets[0] + jnp.arange(KEYS, dtype=jnp.int32)
    keys_t = jnp.transpose(keys, (1, 0, 2))
    values_t = jnp.transpose(values, (1, 0, 2))
    grad_k_sum = jnp.zeros((H, KEYS, HD), jnp.float32)
    grad_v_sum = jnp.zeros((H, KEYS, HD), jnp.float32)
    grad_q_list = []
    for block in range(QBLOCKS):
        query_pos = block_offsets[1 + block] + jnp.arange(QLEN, dtype=jnp.int32)
        q_t = jnp.transpose(queries[block], (1, 0, 2))
        g_t = jnp.transpose(grad_out[block], (1, 0, 2))

        def one_head(items):
            return head_backward(items[0], items[1], items[2], items[3], query_pos, key_pos)

        grad_q, grad_k, grad_v = lax.map(one_head, (q_t, g_t, keys_t, values_t))
        grad_q_list.append(jnp.transpose(grad_q, (1, 0, 2)))
        grad_k_sum = grad_k_sum + grad_k
        grad_v_sum = grad_v_sum + grad_v
    grad_queries = jnp.stack(grad_q_list, axis=0)
    grad_keys = jnp.transpose(grad_k_sum, (1, 0, 2)).astype(jnp.bfloat16)
    grad_values = jnp.transpose(grad_v_sum, (1, 0, 2)).astype(jnp.bfloat16)
    return grad_queries, grad_keys, grad_values
```

```python
import functools
import math

import jax
import jax.numpy as jnp
from jax import lax
from jax.experimental import pallas as pl
from jax.experimental.pallas import tpu as pltpu
from jax.sharding import PartitionSpec as P

MESH = pl.DeviceIdType.MESH
GROUP = 16
STEPS = ((1, 1), (0, 1), (1, 0), (0, 0))


def nt_dot(a, b):
    return lax.dot_general(a, b, (((1,), (1,)), ((), ())), preferred_element_type=jnp.float32)


def swap(x):
    return jnp.transpose(x.astype(jnp.float32), (1, 0, 2)).astype(jnp.bfloat16)


def kernel(
    offs, q_hbm, g_hbm, k_hbm, v_hbm, gq_out, gk_out, gv_out,
    q_in, g_in, k_ref, v_ref, kt_ref,
    send_a, recv_a, send_q, recv_q, send_kv, recv_kv,
    s_ref, dp_ref, pb_ref, gk_acc, gv_acc,
    in_sem, send_sem, recv_a_sem, recv_q_sem, recv_kv_sem,
):
    devices = send_a.shape[0]
    toks = q_in.shape[0]
    half = toks // 2
    key_len, hd = k_ref.shape
    tile = 256
    tiles = key_len // tile
    rows = GROUP * toks
    scale = hd ** -0.5

    me = lax.axis_index("seq")
    group, pos = me // GROUP, me % GROUP
    gy, gh = group // 2, group % 2

    def group_of(dy, dh):
        return lax.rem(gy + dy, 2) * 2 + lax.rem(gh + dh, 2)

    loads = [
        pltpu.make_async_copy(src, dst, in_sem.at[i])
        for i, (src, dst) in enumerate(
            ((q_hbm, q_in), (g_hbm, g_in), (k_hbm, k_ref), (v_hbm, v_ref))
        )
    ]
    for load in loads:
        load.start()

    barrier = pltpu.get_barrier_semaphore()

    def greet(i, carry):
        pl.semaphore_signal(
            barrier, inc=1, device_id={"seq": lax.rem(me + i, devices)}, device_id_type=MESH
        )
        return carry

    lax.fori_loop(1, devices, greet, 0)
    loads[0].wait()
    loads[1].wait()

    def exchange(step, target, src, dst, s_sem, r_sem, own):
        def one(i, carry):
            other = lax.rem(pos + i, GROUP)
            dev = target * GROUP + other
            pltpu.make_async_remote_copy(
                src_ref=src(dev, other), dst_ref=dst, send_sem=s_sem, recv_sem=r_sem,
                device_id={"seq": dev}, device_id_type=MESH,
            ).start()
            return carry

        if own:
            pltpu.make_async_copy(src(me, pos), dst, r_sem).start()
        lax.fori_loop(1 if own else 0, GROUP, one, 0)

    for step, (dy, dh) in enumerate(STEPS):
        target = group_of(dy, dh)
        heads = pl.ds(pl.multiple_of(target * GROUP, GROUP), GROUP)
        send_a[heads, 0:toks, :] = swap(q_in[:, heads, :])
        send_a[heads, toks : 2 * toks, :] = swap(g_in[:, heads, :])
        if step == 0:
            pl.semaphore_wait(barrier, devices - 1)
        exchange(
            step, target, lambda dev, other: send_a.at[dev], recv_a.at[step, pos],
            send_sem.at[0], recv_a_sem.at[step], step == 3,
        )

    loads[2].wait()
    loads[3].wait()
    for t in range(tiles):
        span = pl.ds(t * tile, tile)
        kt_ref[:, span] = jnp.transpose(k_ref[span, :].astype(jnp.float32)).astype(jnp.bfloat16)
    gk_acc[...] = jnp.zeros_like(gk_acc)
    gv_acc[...] = jnp.zeros_like(gv_acc)

    lane = lax.broadcasted_iota(jnp.int32, (1, rows), 1)
    sub = lax.broadcasted_iota(jnp.int32, (tile, rows), 0)
    in_tok = lane % toks
    shift = jnp.where(in_tok >= half, offs[2], offs[1]) - offs[0]
    local_pos = shift + (lane // toks) * half + in_tok % half

    for step, (dy, dh) in enumerate(STEPS):
        source = group_of(dy, dh)
        pltpu.make_async_copy(recv_a.at[step], recv_a.at[step], recv_a_sem.at[step]).wait()
        q = recv_a[step, :, 0:toks, :].reshape(rows, hd)
        g = recv_a[step, :, toks : 2 * toks, :].reshape(rows, hd)
        limit = local_pos + source * (GROUP * half)
        top = jnp.full((1, rows), -jnp.inf, jnp.float32)
        for t in range(tiles):
            span = pl.ds(t * tile, tile)
            s = nt_dot(k_ref[span, :], q)
            s = jnp.where(sub + t * tile <= limit, s, -jnp.inf)
            s_ref[span, :] = s
            top = jnp.maximum(top, jnp.max(s, axis=0, keepdims=True))
        total = jnp.zeros((1, rows), jnp.float32)
        for t in range(tiles):
            span = pl.ds(t * tile, tile)
            e = jnp.exp2((s_ref[span, :] - top) * (scale * math.log2(math.e)))
            s_ref[span, :] = e
            total = total + jnp.sum(e, axis=0, keepdims=True)
        inv = 1.0 / total
        delta = jnp.zeros((1, rows), jnp.float32)
        for t in range(tiles):
            span = pl.ds(t * tile, tile)
            p = s_ref[span, :] * inv
            pb = p.astype(jnp.bfloat16)
            dp = nt_dot(v_ref[span, :], g)
            s_ref[span, :] = p
            pb_ref[span, :] = pb
            dp_ref[span, :] = dp
            delta = delta + jnp.sum(pb.astype(jnp.float32) * dp, axis=0, keepdims=True)
        gq_t = jnp.zeros((hd, rows), jnp.float32)
        for t in range(tiles):
            span = pl.ds(t * tile, tile)
            ds = (s_ref[span, :] * (dp_ref[span, :] - delta)).astype(jnp.bfloat16)
            gq_t = gq_t + jnp.dot(kt_ref[:, span], ds, preferred_element_type=jnp.float32)
            gk_acc[span, :] += jnp.dot(ds, q, preferred_element_type=jnp.float32)
            gv_acc[span, :] += jnp.dot(pb_ref[span, :], g, preferred_element_type=jnp.float32)
        gq = jnp.transpose(gq_t * scale).astype(jnp.bfloat16)
        send_q[step] = gq.reshape(GROUP, toks, hd)
        exchange(
            step, source, lambda dev, other: send_q.at[step, other], recv_q.at[me],
            send_sem.at[1], recv_q_sem, step == 3,
        )

    for step, (dy, dh) in enumerate(STEPS):
        target = group_of(dy, dh)
        span = pl.ds(pl.multiple_of(target * rows, rows), rows)
        owners = pl.ds(target * GROUP, GROUP)
        send_kv[owners, 0:toks, :] = (
            (gk_acc[span, :] * scale).astype(jnp.bfloat16).reshape(GROUP, toks, hd)
        )
        send_kv[owners, toks : 2 * toks, :] = (
            gv_acc[span, :].astype(jnp.bfloat16).reshape(GROUP, toks, hd)
        )
        exchange(
            step, target, lambda dev, other: send_kv.at[dev], recv_kv.at[me],
            send_sem.at[2], recv_kv_sem.at[step], step == 3,
        )

    pltpu.make_async_copy(recv_q, recv_q, recv_q_sem).wait()
    for i in range(devices // GROUP):
        heads = pl.ds(i * GROUP, GROUP)
        gq_out[:, heads, :] = swap(recv_q[heads, :, :])
    for step, (dy, dh) in enumerate(STEPS):
        source = group_of(dy, dh)
        heads = pl.ds(pl.multiple_of(source * GROUP, GROUP), GROUP)
        pltpu.make_async_copy(
            recv_kv.at[heads], recv_kv.at[heads], recv_kv_sem.at[step]
        ).wait()
        gk_out[:, heads, :] = swap(recv_kv[heads, 0:toks, :])
        gv_out[:, heads, :] = swap(recv_kv[heads, toks : 2 * toks, :])
    for i, buf in enumerate((send_a, recv_q, send_kv)):
        sent = buf.at[pl.ds(0, devices - 1)]
        pltpu.make_async_copy(sent, sent, send_sem.at[i]).wait()


def body(queries, grad_out, keys, values, block_offsets):
    blocks, tok, heads, hd = queries.shape
    key_len = keys.shape[0]
    toks = blocks * tok
    rows = GROUP * toks
    bf16, f32 = jnp.bfloat16, jnp.float32
    vmem = pl.BlockSpec(memory_space=pltpu.VMEM)
    hbm = pl.BlockSpec(memory_space=pl.ANY)
    out = jax.ShapeDtypeStruct((toks, heads, hd), bf16)
    gq, gk, gv = pl.pallas_call(
        kernel,
        out_shape=(out, out, out),
        in_specs=[pl.BlockSpec(memory_space=pltpu.SMEM), hbm, hbm, hbm, hbm],
        out_specs=(vmem, vmem, vmem),
        scratch_shapes=[
            pltpu.VMEM((toks, heads, hd), bf16),
            pltpu.VMEM((toks, heads, hd), bf16),
            pltpu.VMEM((key_len, hd), bf16),
            pltpu.VMEM((key_len, hd), bf16),
            pltpu.VMEM((hd, key_len), bf16),
            pltpu.VMEM((heads, 2 * toks, hd), bf16),
            pltpu.VMEM((heads // GROUP, GROUP, 2 * toks, hd), bf16),
            pltpu.VMEM((heads // GROUP, GROUP, toks, hd), bf16),
            pltpu.VMEM((heads, toks, hd), bf16),
            pltpu.VMEM((heads, 2 * toks, hd), bf16),
            pltpu.VMEM((heads, 2 * toks, hd), bf16),
            pltpu.VMEM((key_len, rows), f32),
            pltpu.VMEM((key_len, rows), f32),
            pltpu.VMEM((key_len, rows), bf16),
            pltpu.VMEM((key_len, hd), f32),
            pltpu.VMEM((key_len, hd), f32),
            pltpu.SemaphoreType.DMA((4,)),
            pltpu.SemaphoreType.DMA((3,)),
            pltpu.SemaphoreType.DMA((4,)),
            pltpu.SemaphoreType.DMA,
            pltpu.SemaphoreType.DMA((4,)),
        ],
        compiler_params=pltpu.CompilerParams(
            collective_id=0, has_side_effects=True, vmem_limit_bytes=32 << 20
        ),
        cost_estimate=pl.CostEstimate(
            flops=12 * blocks * tok * heads * key_len * hd,
            bytes_accessed=14 * toks * heads * hd,
            transcendentals=blocks * tok * heads * key_len,
        ),
        name="backward",
    )(
        block_offsets,
        queries.reshape(toks, heads, hd),
        grad_out.reshape(toks, heads, hd),
        keys.reshape(key_len, hd),
        values.reshape(key_len, hd),
    )
    return gq.reshape(blocks, tok, heads, hd), gk, gv


def solution(mesh):
    in_specs = (
        P("batch", "seq", None, None),
        P("batch", "seq", None, None),
        P("batch", "seq", None),
        P("batch", "seq", None),
        P("batch"),
    )
    out_specs = (
        P("batch", "seq", None, None),
        P(("batch", "seq"), None, None),
        P(("batch", "seq"), None, None),
    )
    return jax.shard_map(body, mesh=mesh, in_specs=in_specs, out_specs=out_specs, check_vma=False)
```

```python
import functools
import math

import jax
import jax.numpy as jnp
from jax import lax
from jax.experimental import pallas as pl
from jax.experimental.pallas import tpu as pltpu
from jax.sharding import PartitionSpec as P

MESH = pl.DeviceIdType.MESH
GROUP = 16
STEPS = ((1, 1), (0, 1), (1, 0), (0, 0))
ASTEPS = ((1, 0), (1, 1), (0, 1), (0, 0))
MIB = 1 << 20


def nt_dot(a, b):
    return lax.dot_general(a, b, (((1,), (1,)), ((), ())), preferred_element_type=jnp.float32)


def swap(x):
    return jnp.transpose(x.astype(jnp.float32), (1, 0, 2)).astype(jnp.bfloat16)


def kernel(
    offs_hbm, q_hbm, g_hbm, k_hbm, v_hbm, out_hbm,
    offs, q_in, g_in, k_ref, v_ref, kt_ref,
    send_a, recv_a, send_q, recv_q, send_kv, recv_kv, gq_out, gk_out, gv_out,
    s_ref, dp_ref, pb_ref, gk_acc, gv_acc,
    in_sem, send_sem, recv_a_sem, recv_q_sem, recv_kv_sem, out_sem,
):
    devices = send_a.shape[0]
    toks = q_in.shape[0]
    half = toks // 2
    key_len, hd = k_ref.shape
    tile = 256
    tiles = key_len // tile
    rows = GROUP * toks
    scale = hd ** -0.5

    me = lax.axis_index("seq")
    group, pos = me // GROUP, me % GROUP
    gy, gh = group // 2, group % 2

    def group_of(dy, dh):
        return lax.rem(gy + dy, 2) * 2 + lax.rem(gh + dh, 2)

    barrier = pltpu.get_barrier_semaphore()
    for step, (dy, dh) in enumerate(STEPS):
        target = group_of(dy, dh)

        def greet(i, carry):
            pl.semaphore_signal(
                barrier, inc=1, device_id={"seq": target * GROUP + lax.rem(pos + i, GROUP)},
                device_id_type=MESH,
            )
            return carry

        lax.fori_loop(1 if step == 3 else 0, GROUP, greet, 0)

    loads = [
        pltpu.make_async_copy(src, dst, in_sem.at[i])
        for i, (src, dst) in enumerate(
            ((q_hbm, q_in), (g_hbm, g_in), (k_hbm, k_ref), (v_hbm, v_ref), (offs_hbm, offs))
        )
    ]
    for load in loads:
        load.start()
    loads[0].wait()
    loads[1].wait()

    def exchange(step, target, src, dst, s_sem, r_sem, own):
        def one(i, carry):
            other = lax.rem(pos + i, GROUP)
            dev = target * GROUP + other
            pltpu.make_async_remote_copy(
                src_ref=src(dev, other), dst_ref=dst, send_sem=s_sem, recv_sem=r_sem,
                device_id={"seq": dev}, device_id_type=MESH,
            ).start()
            return carry

        if own:
            pltpu.make_async_copy(src(me, pos), dst, r_sem).start()
        lax.fori_loop(1 if own else 0, GROUP, one, 0)

    for step, (dy, dh) in enumerate(ASTEPS):
        target = group_of(dy, dh)
        heads = pl.ds(pl.multiple_of(target * GROUP, GROUP), GROUP)
        send_a[heads, 0:toks, :] = swap(q_in[:, heads, :])
        send_a[heads, toks : 2 * toks, :] = swap(g_in[:, heads, :])
        if step == 0:
            pl.semaphore_wait(barrier, devices - 1)
        exchange(
            step, target, lambda dev, other: send_a.at[dev], recv_a.at[step, pos],
            send_sem.at[0], recv_a_sem.at[step], step == 3,
        )

    for load in loads[2:]:
        load.wait()
    for t in range(tiles):
        span = pl.ds(t * tile, tile)
        kt_ref[:, span] = jnp.transpose(k_ref[span, :].astype(jnp.float32)).astype(jnp.bfloat16)
    gk_acc[...] = jnp.zeros_like(gk_acc)
    gv_acc[...] = jnp.zeros_like(gv_acc)

    lane = lax.broadcasted_iota(jnp.int32, (1, rows), 1)
    sub = lax.broadcasted_iota(jnp.int32, (tile, rows), 0)
    in_tok = lane % toks
    shift = jnp.where(in_tok >= half, offs[2], offs[1]) - offs[0]
    local_pos = shift + (lane // toks) * half + in_tok % half

    for step, (dy, dh) in enumerate(ASTEPS):
        source = group_of(dy, dh)
        pltpu.make_async_copy(recv_a.at[step], recv_a.at[step], recv_a_sem.at[step]).wait()
        q = recv_a[step, :, 0:toks, :].reshape(rows, hd)
        g = recv_a[step, :, toks : 2 * toks, :].reshape(rows, hd)
        limit = local_pos + source * (GROUP * half)
        top = jnp.full((1, rows), -jnp.inf, jnp.float32)
        for t in range(tiles):
            span = pl.ds(t * tile, tile)
            s = nt_dot(k_ref[span, :], q)
            s = jnp.where(sub + t * tile <= limit, s, -jnp.inf)
            s_ref[span, :] = s
            top = jnp.maximum(top, jnp.max(s, axis=0, keepdims=True))
        total = jnp.zeros((1, rows), jnp.float32)
        for t in range(tiles):
            span = pl.ds(t * tile, tile)
            e = jnp.exp2((s_ref[span, :] - top) * (scale * math.log2(math.e)))
            s_ref[span, :] = e
            total = total + jnp.sum(e, axis=0, keepdims=True)
        inv = 1.0 / total
        delta = jnp.zeros((1, rows), jnp.float32)
        for t in range(tiles):
            span = pl.ds(t * tile, tile)
            p = s_ref[span, :] * inv
            pb = p.astype(jnp.bfloat16)
            dp = nt_dot(v_ref[span, :], g)
            s_ref[span, :] = p
            pb_ref[span, :] = pb
            dp_ref[span, :] = dp
            delta = delta + jnp.sum(pb.astype(jnp.float32) * dp, axis=0, keepdims=True)
        gq_t = jnp.zeros((hd, rows), jnp.float32)
        for t in range(tiles):
            span = pl.ds(t * tile, tile)
            ds = (s_ref[span, :] * (dp_ref[span, :] - delta)).astype(jnp.bfloat16)
            gq_t = gq_t + jnp.dot(kt_ref[:, span], ds, preferred_element_type=jnp.float32)
            gk_acc[span, :] += jnp.dot(ds, q, preferred_element_type=jnp.float32)
            gv_acc[span, :] += jnp.dot(pb_ref[span, :], g, preferred_element_type=jnp.float32)
        gq = jnp.transpose(gq_t * scale).astype(jnp.bfloat16)
        send_q[step] = gq.reshape(GROUP, toks, hd)
        exchange(
            step, source, lambda dev, other: send_q.at[step, other], recv_q.at[me],
            send_sem.at[1], recv_q_sem, step == 3,
        )

    for step, (dy, dh) in enumerate(STEPS):
        target = group_of(dy, dh)
        span = pl.ds(pl.multiple_of(target * rows, rows), rows)
        owners = pl.ds(target * GROUP, GROUP)
        send_kv[owners, 0:toks, :] = (
            (gk_acc[span, :] * scale).astype(jnp.bfloat16).reshape(GROUP, toks, hd)
        )
        send_kv[owners, toks : 2 * toks, :] = (
            gv_acc[span, :].astype(jnp.bfloat16).reshape(GROUP, toks, hd)
        )
        exchange(
            step, target, lambda dev, other: send_kv.at[dev], recv_kv.at[me],
            send_sem.at[2], recv_kv_sem.at[step], step == 3,
        )

    stores = []

    def store(i, staged, out, heads):
        stores.append(
            pltpu.make_async_copy(staged.at[:, heads, :], out.at[:, heads, :], out_sem.at[i])
        )
        stores[-1].start()

    pltpu.make_async_copy(recv_q, recv_q, recv_q_sem).wait()
    for i in range(devices // GROUP):
        heads = pl.ds(i * GROUP, GROUP)
        gq_out[:, heads, :] = swap(recv_q[heads, :, :])
        store(i, gq_out, out_hbm.at[0], heads)
    for step, (dy, dh) in enumerate(STEPS):
        source = group_of(dy, dh)
        heads = pl.ds(pl.multiple_of(source * GROUP, GROUP), GROUP)
        pltpu.make_async_copy(
            recv_kv.at[heads], recv_kv.at[heads], recv_kv_sem.at[step]
        ).wait()
        gk_out[:, heads, :] = swap(recv_kv[heads, 0:toks, :])
        store(4 + step, gk_out, out_hbm.at[1], heads)
        gv_out[:, heads, :] = swap(recv_kv[heads, toks : 2 * toks, :])
        store(8 + step, gv_out, out_hbm.at[2], heads)
    for copy in stores:
        copy.wait()
    for i, buf in enumerate((send_a, recv_q, send_kv)):
        sent = buf.at[pl.ds(0, devices - 1)]
        pltpu.make_async_copy(sent, sent, send_sem.at[i]).wait()


def body(queries, grad_out, keys, values, block_offsets):
    blocks, tok, heads, hd = queries.shape
    key_len = keys.shape[0]
    toks = blocks * tok
    rows = GROUP * toks
    bf16, f32 = jnp.bfloat16, jnp.float32
    hbm = pl.BlockSpec(memory_space=pl.ANY)
    grads = pl.pallas_call(
        kernel,
        out_shape=jax.ShapeDtypeStruct((3, toks, heads, hd), bf16),
        in_specs=[hbm] * 5,
        out_specs=hbm,
        scratch_shapes=[
            pltpu.SMEM((1 + blocks,), jnp.int32),
            pltpu.VMEM((toks, heads, hd), bf16),
            pltpu.VMEM((toks, heads, hd), bf16),
            pltpu.VMEM((key_len, hd), bf16),
            pltpu.VMEM((key_len, hd), bf16),
            pltpu.VMEM((hd, key_len), bf16),
            pltpu.VMEM((heads, 2 * toks, hd), bf16),
            pltpu.VMEM((heads // GROUP, GROUP, 2 * toks, hd), bf16),
            pltpu.VMEM((heads // GROUP, GROUP, toks, hd), bf16),
            pltpu.VMEM((heads, toks, hd), bf16),
            pltpu.VMEM((heads, 2 * toks, hd), bf16),
            pltpu.VMEM((heads, 2 * toks, hd), bf16),
            pltpu.VMEM((toks, heads, hd), bf16),
            pltpu.VMEM((toks, heads, hd), bf16),
            pltpu.VMEM((toks, heads, hd), bf16),
            pltpu.VMEM((key_len, rows), f32),
            pltpu.VMEM((key_len, rows), f32),
            pltpu.VMEM((key_len, rows), bf16),
            pltpu.VMEM((key_len, hd), f32),
            pltpu.VMEM((key_len, hd), f32),
            pltpu.SemaphoreType.DMA((5,)),
            pltpu.SemaphoreType.DMA((3,)),
            pltpu.SemaphoreType.DMA((4,)),
            pltpu.SemaphoreType.DMA,
            pltpu.SemaphoreType.DMA((4,)),
            pltpu.SemaphoreType.DMA((12,)),
        ],
        compiler_params=pltpu.CompilerParams(
            collective_id=0, has_side_effects=True, vmem_limit_bytes=60 * MIB
        ),
        cost_estimate=pl.CostEstimate(
            flops=12 * blocks * tok * heads * key_len * hd,
            bytes_accessed=14 * toks * heads * hd,
            transcendentals=blocks * tok * heads * key_len,
        ),
        name="backward",
    )(
        block_offsets,
        queries.reshape(toks, heads, hd),
        grad_out.reshape(toks, heads, hd),
        keys.reshape(key_len, hd),
        values.reshape(key_len, hd),
    )
    return grads[0].reshape(blocks, tok, heads, hd), grads[1], grads[2]


def solution(mesh):
    in_specs = (
        P("batch", "seq", None, None),
        P("batch", "seq", None, None),
        P("batch", "seq", None),
        P("batch", "seq", None),
        P("batch"),
    )
    out_specs = (
        P("batch", "seq", None, None),
        P(("batch", "seq"), None, None),
        P(("batch", "seq"), None, None),
    )
    return jax.shard_map(body, mesh=mesh, in_specs=in_specs, out_specs=out_specs, check_vma=False)
```

```python
import functools
import math

import jax
import jax.numpy as jnp
from jax import lax
from jax.experimental import pallas as pl
from jax.experimental.pallas import tpu as pltpu
from jax.sharding import PartitionSpec as P

MESH = pl.DeviceIdType.MESH
GROUP = 16
MIB = 1 << 20


def nt_dot(a, b):
    return lax.dot_general(a, b, (((1,), (1,)), ((), ())), preferred_element_type=jnp.float32)


def swap(x):
    return jnp.transpose(x.astype(jnp.float32), (1, 0, 2)).astype(jnp.bfloat16)


def kernel(
    offs_hbm, q_hbm, g_hbm, k_hbm, v_hbm, out_hbm,
    offs, q_in, g_in, k_ref, v_ref, kt_ref,
    send_a, recv_a, send_q, recv_q, send_kv, recv_kv, gq_out, gk_out, gv_out,
    s_ref, dp_ref, pb_ref, gk_acc, gv_acc,
    in_sem, send_sem, recv_a_sem, recv_q_sem, recv_kv_sem, out_sem,
):
    devices = send_a.shape[0]
    toks = q_in.shape[0]
    half = toks // 2
    key_len, hd = k_ref.shape
    tile = 256
    tiles = key_len // tile
    rows = GROUP * toks
    scale = hd ** -0.5

    me = lax.axis_index("seq")
    slots = devices // GROUP
    ring = devices // 4
    my_y, my_z, my_c = me // (2 * ring), (me // 2) % ring, me % 2

    def partner(slot, i, sign):
        p = (slot % 2) * (GROUP // 2) + i // 2
        dz = (1 - p % 2) * (ring // 2 + p // 2) + (p % 2) * (ring // 2 - (p + 1) // 2)
        y = 1 - my_y if slot < 2 else my_y
        z = (my_z + ring + sign * dz) % ring
        c = (my_c + 1 + i % 2) % 2
        return (y * ring + z) * 2 + c

    barrier = pltpu.get_barrier_semaphore()
    for slot in range(slots):

        def greet(i, carry):
            pl.semaphore_signal(
                barrier, inc=1, device_id={"seq": partner(slot, i, 1)}, device_id_type=MESH
            )
            return carry

        lax.fori_loop(0, GROUP - (slot == slots - 1), greet, 0)

    loads = [
        pltpu.make_async_copy(src, dst, in_sem.at[i])
        for i, (src, dst) in enumerate(
            ((q_hbm, q_in), (g_hbm, g_in), (k_hbm, k_ref), (v_hbm, v_ref), (offs_hbm, offs))
        )
    ]
    for load in loads:
        load.start()
    loads[0].wait()
    loads[1].wait()

    def exchange(slot, sign, src, dst, s_sem, r_sem):
        def one(i, carry):
            dev = partner(slot, i, sign)
            pltpu.make_async_remote_copy(
                src_ref=src(dev, i), dst_ref=dst(i), send_sem=s_sem, recv_sem=r_sem,
                device_id={"seq": dev}, device_id_type=MESH,
            ).start()
            return carry

        own = slot == slots - 1
        lax.fori_loop(0, GROUP - own, one, 0)
        if own:
            pltpu.make_async_copy(src(me, GROUP - 1), dst(GROUP - 1), r_sem).start()

    for i in range(slots):
        heads = pl.ds(i * GROUP, GROUP)
        send_a[heads, 0:toks, :] = swap(q_in[:, heads, :])
        send_a[heads, toks : 2 * toks, :] = swap(g_in[:, heads, :])
    pl.semaphore_wait(barrier, devices - 1)
    for slot in range(slots):
        exchange(
            slot, 1, lambda dev, i: send_a.at[dev], lambda i: recv_a.at[slot, i],
            send_sem.at[0], recv_a_sem.at[slot],
        )

    for load in loads[2:]:
        load.wait()
    for t in range(tiles):
        span = pl.ds(t * tile, tile)
        kt_ref[:, span] = jnp.transpose(k_ref[span, :].astype(jnp.float32)).astype(jnp.bfloat16)
    gk_acc[...] = jnp.zeros_like(gk_acc)
    gv_acc[...] = jnp.zeros_like(gv_acc)

    lane = lax.broadcasted_iota(jnp.int32, (1, rows), 1)
    sub = lax.broadcasted_iota(jnp.int32, (tile, rows), 0)
    in_tok = lane % toks
    shift = jnp.where(in_tok >= half, offs[2], offs[1]) - offs[0]
    local_pos = shift + in_tok % half

    for step in range(slots):
        pltpu.make_async_copy(recv_a.at[step], recv_a.at[step], recv_a_sem.at[step]).wait()
        q = recv_a[step, :, 0:toks, :].reshape(rows, hd)
        g = recv_a[step, :, toks : 2 * toks, :].reshape(rows, hd)
        limit = local_pos + half * partner(step, lane // toks, -1)
        top = jnp.full((1, rows), -jnp.inf, jnp.float32)
        for t in range(tiles):
            span = pl.ds(t * tile, tile)
            s = nt_dot(k_ref[span, :], q)
            s = jnp.where(sub + t * tile <= limit, s, -jnp.inf)
            s_ref[span, :] = s
            top = jnp.maximum(top, jnp.max(s, axis=0, keepdims=True))
        total = jnp.zeros((1, rows), jnp.float32)
        for t in range(tiles):
            span = pl.ds(t * tile, tile)
            e = jnp.exp2((s_ref[span, :] - top) * (scale * math.log2(math.e)))
            s_ref[span, :] = e
            total = total + jnp.sum(e, axis=0, keepdims=True)
        inv = 1.0 / total
        delta = jnp.zeros((1, rows), jnp.float32)
        for t in range(tiles):
            span = pl.ds(t * tile, tile)
            p = s_ref[span, :] * inv
            pb = p.astype(jnp.bfloat16)
            dp = nt_dot(v_ref[span, :], g)
            s_ref[span, :] = p
            pb_ref[span, :] = pb
            dp_ref[span, :] = dp
            delta = delta + jnp.sum(pb.astype(jnp.float32) * dp, axis=0, keepdims=True)
        gq_t = jnp.zeros((hd, rows), jnp.float32)
        for t in range(tiles):
            span = pl.ds(t * tile, tile)
            ds = (s_ref[span, :] * (dp_ref[span, :] - delta)).astype(jnp.bfloat16)
            gq_t = gq_t + jnp.dot(kt_ref[:, span], ds, preferred_element_type=jnp.float32)
            gk_acc[span, :] += jnp.dot(ds, q, preferred_element_type=jnp.float32)
            gv_acc[span, :] += jnp.dot(pb_ref[span, :], g, preferred_element_type=jnp.float32)
        gq = jnp.transpose(gq_t * scale).astype(jnp.bfloat16)
        send_q[step] = gq.reshape(GROUP, toks, hd)
        exchange(
            step, -1, lambda dev, i: send_q.at[step, i], lambda i: recv_q.at[me],
            send_sem.at[1], recv_q_sem,
        )

    for i in range(slots):
        span = pl.ds(i * rows, rows)
        owners = pl.ds(i * GROUP, GROUP)
        send_kv[owners, 0:toks, :] = (
            (gk_acc[span, :] * scale).astype(jnp.bfloat16).reshape(GROUP, toks, hd)
        )
        send_kv[owners, toks : 2 * toks, :] = (
            gv_acc[span, :].astype(jnp.bfloat16).reshape(GROUP, toks, hd)
        )
    group = me // GROUP
    for slot in range(slots):
        exchange(
            slot, 1, lambda dev, i: send_kv.at[dev], lambda i: recv_kv.at[me],
            send_sem.at[2], recv_kv_sem.at[group],
        )

    stores = []

    def store(i, staged, out, heads):
        stores.append(
            pltpu.make_async_copy(staged.at[:, heads, :], out.at[:, heads, :], out_sem.at[i])
        )
        stores[-1].start()

    pltpu.make_async_copy(recv_q, recv_q, recv_q_sem).wait()
    for i in range(devices // GROUP):
        heads = pl.ds(i * GROUP, GROUP)
        gq_out[:, heads, :] = swap(recv_q[heads, :, :])
        store(i, gq_out, out_hbm.at[0], heads)
    for step, ahead in enumerate((2, 3, 1, 0)):
        source = (group // 2 + ahead // 2) % 2 * 2 + (group + ahead) % 2
        heads = pl.ds(pl.multiple_of(source * GROUP, GROUP), GROUP)
        pltpu.make_async_copy(
            recv_kv.at[heads], recv_kv.at[heads], recv_kv_sem.at[source]
        ).wait()
        gk_out[:, heads, :] = swap(recv_kv[heads, 0:toks, :])
        store(4 + step, gk_out, out_hbm.at[1], heads)
        gv_out[:, heads, :] = swap(recv_kv[heads, toks : 2 * toks, :])
        store(8 + step, gv_out, out_hbm.at[2], heads)
    for copy in stores:
        copy.wait()
    for i, buf in enumerate((send_a, recv_q, send_kv)):
        sent = buf.at[pl.ds(0, devices - 1)]
        pltpu.make_async_copy(sent, sent, send_sem.at[i]).wait()


def body(queries, grad_out, keys, values, block_offsets):
    blocks, tok, heads, hd = queries.shape
    key_len = keys.shape[0]
    toks = blocks * tok
    rows = GROUP * toks
    bf16, f32 = jnp.bfloat16, jnp.float32
    hbm = pl.BlockSpec(memory_space=pl.ANY)
    grads = pl.pallas_call(
        kernel,
        out_shape=jax.ShapeDtypeStruct((3, toks, heads, hd), bf16),
        in_specs=[hbm] * 5,
        out_specs=hbm,
        scratch_shapes=[
            pltpu.SMEM((1 + blocks,), jnp.int32),
            pltpu.VMEM((toks, heads, hd), bf16),
            pltpu.VMEM((toks, heads, hd), bf16),
            pltpu.VMEM((key_len, hd), bf16),
            pltpu.VMEM((key_len, hd), bf16),
            pltpu.VMEM((hd, key_len), bf16),
            pltpu.VMEM((heads, 2 * toks, hd), bf16),
            pltpu.VMEM((heads // GROUP, GROUP, 2 * toks, hd), bf16),
            pltpu.VMEM((heads // GROUP, GROUP, toks, hd), bf16),
            pltpu.VMEM((heads, toks, hd), bf16),
            pltpu.VMEM((heads, 2 * toks, hd), bf16),
            pltpu.VMEM((heads, 2 * toks, hd), bf16),
            pltpu.VMEM((toks, heads, hd), bf16),
            pltpu.VMEM((toks, heads, hd), bf16),
            pltpu.VMEM((toks, heads, hd), bf16),
            pltpu.VMEM((key_len, rows), f32),
            pltpu.VMEM((key_len, rows), f32),
            pltpu.VMEM((key_len, rows), bf16),
            pltpu.VMEM((key_len, hd), f32),
            pltpu.VMEM((key_len, hd), f32),
            pltpu.SemaphoreType.DMA((5,)),
            pltpu.SemaphoreType.DMA((3,)),
            pltpu.SemaphoreType.DMA((4,)),
            pltpu.SemaphoreType.DMA,
            pltpu.SemaphoreType.DMA((4,)),
            pltpu.SemaphoreType.DMA((12,)),
        ],
        compiler_params=pltpu.CompilerParams(
            collective_id=0, has_side_effects=True, vmem_limit_bytes=60 * MIB
        ),
        cost_estimate=pl.CostEstimate(
            flops=12 * blocks * tok * heads * key_len * hd,
            bytes_accessed=14 * toks * heads * hd,
            transcendentals=blocks * tok * heads * key_len,
        ),
        name="backward",
    )(
        block_offsets,
        queries.reshape(toks, heads, hd),
        grad_out.reshape(toks, heads, hd),
        keys.reshape(key_len, hd),
        values.reshape(key_len, hd),
    )
    return grads[0].reshape(blocks, tok, heads, hd), grads[1], grads[2]


def solution(mesh):
    in_specs = (
        P("batch", "seq", None, None),
        P("batch", "seq", None, None),
        P("batch", "seq", None),
        P("batch", "seq", None),
        P("batch"),
    )
    out_specs = (
        P("batch", "seq", None, None),
        P(("batch", "seq"), None, None),
        P(("batch", "seq"), None, None),
    )
    return jax.shard_map(body, mesh=mesh, in_specs=in_specs, out_specs=out_specs, check_vma=False)
```

```python
import functools
import math

import jax
import jax.numpy as jnp
from jax import lax
from jax.experimental import pallas as pl
from jax.experimental.pallas import tpu as pltpu
from jax.sharding import PartitionSpec as P

MESH = pl.DeviceIdType.MESH
GROUP = 16
MIB = 1 << 20


def nt_dot(a, b):
    return lax.dot_general(a, b, (((1,), (1,)), ((), ())), preferred_element_type=jnp.float32)


def swap(x):
    return jnp.transpose(x.astype(jnp.float32), (1, 0, 2)).astype(jnp.bfloat16)


def kernel(
    offs_hbm, q_hbm, g_hbm, k_hbm, v_hbm, gq_hbm, recv_kv,
    offs, q_in, g_in, k_ref, v_ref, kt_ref,
    send_a, recv_a, send_q, recv_q, send_kv, gq_out,
    s_ref, dp_ref, pb_ref, gk_acc, gv_acc,
    in_sem, send_sem, recv_a_sem, recv_q_sem, recv_kv_sem, out_sem,
):
    devices = send_a.shape[0]
    toks = q_in.shape[0]
    half = toks // 2
    key_len, hd = k_ref.shape
    tile = 256
    tiles = key_len // tile
    rows = GROUP * toks
    scale = hd ** -0.5

    me = lax.axis_index("seq")
    slots = devices // GROUP
    ring = devices // 4
    my_y, my_z, my_c = me // (2 * ring), (me // 2) % ring, me % 2

    def partner(slot, j, m, sign):
        k = (slot % 2) * (GROUP // 4) + j
        dz = ring // 2 + k if m < 2 else ring // 2 - 1 - k
        y = 1 - my_y if slot < 2 else my_y
        z = lax.rem(my_z + dz if sign > 0 else my_z + ring - dz, ring)
        c = 1 - my_c if m % 2 == 0 else my_c
        return (y * ring + z) * 2 + c

    def each(slot, sign, act):
        def four(j, carry):
            for m in range(4):
                act(partner(slot, j, m, sign), 4 * j + m)
            return carry

        last = GROUP // 4 - 1
        if slot < slots - 1:
            lax.fori_loop(0, last + 1, four, 0)
        else:
            lax.fori_loop(0, last, four, 0)
            for m in range(3):
                act(partner(slot, last, m, sign), 4 * last + m)

    barrier = pltpu.get_barrier_semaphore()
    for slot in range(slots):
        each(slot, 1, lambda dev, i: pl.semaphore_signal(
            barrier, inc=1, device_id={"seq": dev}, device_id_type=MESH
        ))

    loads = [
        pltpu.make_async_copy(src, dst, in_sem.at[i])
        for i, (src, dst) in enumerate(
            ((q_hbm, q_in), (g_hbm, g_in), (k_hbm, k_ref), (v_hbm, v_ref), (offs_hbm, offs))
        )
    ]
    for load in loads:
        load.start()
    loads[0].wait()
    loads[1].wait()

    def exchange(slot, sign, src, dst, s_sem, r_sem):
        def one(dev, i):
            pltpu.make_async_remote_copy(
                src_ref=src(dev, i), dst_ref=dst(i), send_sem=s_sem, recv_sem=r_sem,
                device_id={"seq": dev}, device_id_type=MESH,
            ).start()

        each(slot, sign, one)
        if slot == slots - 1:
            pltpu.make_async_copy(src(me, GROUP - 1), dst(GROUP - 1), r_sem).start()

    for i in range(slots):
        heads = pl.ds(i * GROUP, GROUP)
        send_a[heads, 0:toks, :] = swap(q_in[:, heads, :])
        send_a[heads, toks : 2 * toks, :] = swap(g_in[:, heads, :])
    pl.semaphore_wait(barrier, devices - 1)
    for slot in range(slots):
        exchange(
            slot, 1, lambda dev, i: send_a.at[dev], lambda i: recv_a.at[slot, i],
            send_sem.at[0], recv_a_sem.at[slot],
        )

    for load in loads[2:]:
        load.wait()
    for t in range(tiles):
        span = pl.ds(t * tile, tile)
        kt_ref[:, span] = jnp.transpose(k_ref[span, :].astype(jnp.float32)).astype(jnp.bfloat16)
    gk_acc[...] = jnp.zeros_like(gk_acc)
    gv_acc[...] = jnp.zeros_like(gv_acc)

    lane = lax.broadcasted_iota(jnp.int32, (1, rows), 1)
    sub = lax.broadcasted_iota(jnp.int32, (tile, rows), 0)
    in_tok = lane % toks
    number = lane // toks
    shift = jnp.where(in_tok >= half, offs[2], offs[1]) - offs[0]
    local_pos = shift + in_tok % half

    for step in range(slots):
        pltpu.make_async_copy(recv_a.at[step], recv_a.at[step], recv_a_sem.at[step]).wait()
        q = recv_a[step, :, 0:toks, :].reshape(rows, hd)
        g = recv_a[step, :, toks : 2 * toks, :].reshape(rows, hd)
        device = jnp.zeros_like(lane)
        for m in range(4):
            device = jnp.where(number % 4 == m, partner(step, number // 4, m, -1), device)
        limit = local_pos + half * device
        top = jnp.full((1, rows), -jnp.inf, jnp.float32)
        for t in range(tiles):
            span = pl.ds(t * tile, tile)
            s = nt_dot(k_ref[span, :], q)
            s = jnp.where(sub + t * tile <= limit, s, -jnp.inf)
            s_ref[span, :] = s
            top = jnp.maximum(top, jnp.max(s, axis=0, keepdims=True))
        total = jnp.zeros((1, rows), jnp.float32)
        for t in range(tiles):
            span = pl.ds(t * tile, tile)
            e = jnp.exp2((s_ref[span, :] - top) * (scale * math.log2(math.e)))
            s_ref[span, :] = e
            total = total + jnp.sum(e, axis=0, keepdims=True)
        inv = 1.0 / total
        delta = jnp.zeros((1, rows), jnp.float32)
        for t in range(tiles):
            span = pl.ds(t * tile, tile)
            p = s_ref[span, :] * inv
            pb = p.astype(jnp.bfloat16)
            dp = nt_dot(v_ref[span, :], g)
            s_ref[span, :] = p
            pb_ref[span, :] = pb
            dp_ref[span, :] = dp
            delta = delta + jnp.sum(pb.astype(jnp.float32) * dp, axis=0, keepdims=True)
        gq_t = jnp.zeros((hd, rows), jnp.float32)
        for t in range(tiles):
            span = pl.ds(t * tile, tile)
            ds = (s_ref[span, :] * (dp_ref[span, :] - delta)).astype(jnp.bfloat16)
            gq_t = gq_t + jnp.dot(kt_ref[:, span], ds, preferred_element_type=jnp.float32)
            gk_acc[span, :] += jnp.dot(ds, q, preferred_element_type=jnp.float32)
            gv_acc[span, :] += jnp.dot(pb_ref[span, :], g, preferred_element_type=jnp.float32)
        gq = jnp.transpose(gq_t * scale).astype(jnp.bfloat16)
        send_q[step] = gq.reshape(GROUP, toks, hd)
        exchange(
            step, -1, lambda dev, i: send_q.at[step, i], lambda i: recv_q.at[me],
            send_sem.at[1], recv_q_sem,
        )

    for i in range(slots):
        span = pl.ds(i * rows, rows)
        owners = pl.ds(i * GROUP, GROUP)
        send_kv[owners, 0:toks, :] = (
            (gk_acc[span, :] * scale).astype(jnp.bfloat16).reshape(GROUP, toks, hd)
        )
        send_kv[owners, toks : 2 * toks, :] = (
            gv_acc[span, :].astype(jnp.bfloat16).reshape(GROUP, toks, hd)
        )
    for slot in range(slots):
        exchange(
            slot, 1, lambda dev, i: send_kv.at[dev], lambda i: recv_kv.at[me],
            send_sem.at[2], recv_kv_sem,
        )

    stores = []

    def store(i, staged, out, heads):
        stores.append(
            pltpu.make_async_copy(staged.at[:, heads, :], out.at[:, heads, :], out_sem.at[i])
        )
        stores[-1].start()

    pltpu.make_async_copy(recv_q, recv_q, recv_q_sem).wait()
    for i in range(devices // GROUP):
        heads = pl.ds(i * GROUP, GROUP)
        gq_out[:, heads, :] = swap(recv_q[heads, :, :])
        store(i, gq_out, gq_hbm, heads)
    pltpu.make_async_copy(recv_kv, recv_kv, recv_kv_sem).wait()
    for copy in stores:
        copy.wait()
    for i, buf in enumerate((send_a, recv_q, send_kv)):
        sent = buf.at[pl.ds(0, devices - 1)]
        pltpu.make_async_copy(sent, sent, send_sem.at[i]).wait()


def by_token(gq_in, kv_in, gq_hbm, gk_hbm, gv_hbm, gq, kv, gk, gv, in_sem, out_sem):
    toks = gq.shape[0]
    slots = kv.shape[0] // GROUP
    groups = [pl.ds(i * GROUP, GROUP) for i in range(slots)]
    loads = [
        pltpu.make_async_copy(kv_in.at[heads], kv.at[heads], in_sem.at[i])
        for i, heads in enumerate(groups)
    ]
    loads.append(pltpu.make_async_copy(gq_in, gq, in_sem.at[slots]))
    for load in loads:
        load.start()
    stores = []

    def store(src, dst):
        stores.append(pltpu.make_async_copy(src, dst, out_sem.at[len(stores)]))
        stores[-1].start()

    for i, heads in enumerate(groups):
        loads[i].wait()
        gk[:, heads, :] = swap(kv[heads, 0:toks, :])
        store(gk.at[:, heads, :], gk_hbm.at[:, heads, :])
        gv[:, heads, :] = swap(kv[heads, toks : 2 * toks, :])
        store(gv.at[:, heads, :], gv_hbm.at[:, heads, :])
        if i == 0:
            loads[slots].wait()
            store(gq, gq_hbm)
    for copy in stores:
        copy.wait()


def body(queries, grad_out, keys, values, block_offsets):
    blocks, tok, heads, hd = queries.shape
    key_len = keys.shape[0]
    toks = blocks * tok
    rows = GROUP * toks
    bf16, f32 = jnp.bfloat16, jnp.float32
    hbm = pl.BlockSpec(memory_space=pl.ANY)
    out = jax.ShapeDtypeStruct((toks, heads, hd), bf16)
    gq, kv = pl.pallas_call(
        kernel,
        out_shape=(out, jax.ShapeDtypeStruct((heads, 2 * toks, hd), bf16)),
        in_specs=[hbm] * 5,
        out_specs=(hbm, hbm),
        scratch_shapes=[
            pltpu.SMEM((1 + blocks,), jnp.int32),
            pltpu.VMEM((toks, heads, hd), bf16),
            pltpu.VMEM((toks, heads, hd), bf16),
            pltpu.VMEM((key_len, hd), bf16),
            pltpu.VMEM((key_len, hd), bf16),
            pltpu.VMEM((hd, key_len), bf16),
            pltpu.VMEM((heads, 2 * toks, hd), bf16),
            pltpu.VMEM((heads // GROUP, GROUP, 2 * toks, hd), bf16),
            pltpu.VMEM((heads // GROUP, GROUP, toks, hd), bf16),
            pltpu.VMEM((heads, toks, hd), bf16),
            pltpu.VMEM((heads, 2 * toks, hd), bf16),
            pltpu.VMEM((toks, heads, hd), bf16),
            pltpu.VMEM((key_len, rows), f32),
            pltpu.VMEM((key_len, rows), f32),
            pltpu.VMEM((key_len, rows), bf16),
            pltpu.VMEM((key_len, hd), f32),
            pltpu.VMEM((key_len, hd), f32),
            pltpu.SemaphoreType.DMA((5,)),
            pltpu.SemaphoreType.DMA((3,)),
            pltpu.SemaphoreType.DMA((4,)),
            pltpu.SemaphoreType.DMA,
            pltpu.SemaphoreType.DMA,
            pltpu.SemaphoreType.DMA((4,)),
        ],
        compiler_params=pltpu.CompilerParams(
            collective_id=0, has_side_effects=True, vmem_limit_bytes=60 * MIB
        ),
        cost_estimate=pl.CostEstimate(
            flops=12 * blocks * tok * heads * key_len * hd,
            bytes_accessed=14 * toks * heads * hd,
            transcendentals=blocks * tok * heads * key_len,
        ),
        name="backward",
    )(
        block_offsets,
        queries.reshape(toks, heads, hd),
        grad_out.reshape(toks, heads, hd),
        keys.reshape(key_len, hd),
        values.reshape(key_len, hd),
    )
    gq, gk, gv = pl.pallas_call(
        by_token,
        out_shape=(out, out, out),
        in_specs=[hbm, hbm],
        out_specs=(hbm, hbm, hbm),
        scratch_shapes=[
            pltpu.VMEM((toks, heads, hd), bf16),
            pltpu.VMEM((heads, 2 * toks, hd), bf16),
            pltpu.VMEM((toks, heads, hd), bf16),
            pltpu.VMEM((toks, heads, hd), bf16),
            pltpu.SemaphoreType.DMA((1 + heads // GROUP,)),
            pltpu.SemaphoreType.DMA((1 + 2 * heads // GROUP,)),
        ],
        name="by_token",
    )(gq, kv)
    return gq.reshape(blocks, tok, heads, hd), gk, gv


def solution(mesh):
    in_specs = (
        P("batch", "seq", None, None),
        P("batch", "seq", None, None),
        P("batch", "seq", None),
        P("batch", "seq", None),
        P("batch"),
    )
    out_specs = (
        P("batch", "seq", None, None),
        P(("batch", "seq"), None, None),
        P(("batch", "seq"), None, None),
    )
    return jax.shard_map(body, mesh=mesh, in_specs=in_specs, out_specs=out_specs, check_vma=False)
```

```python
import functools
import math

import jax
import jax.numpy as jnp
from jax import lax
from jax.experimental import pallas as pl
from jax.experimental.pallas import tpu as pltpu
from jax.sharding import PartitionSpec as P

MESH = pl.DeviceIdType.MESH
GROUP = 16
MIB = 1 << 20


def nt_dot(a, b):
    return lax.dot_general(a, b, (((1,), (1,)), ((), ())), preferred_element_type=jnp.float32)


def swap(x):
    return jnp.transpose(x.astype(jnp.float32), (1, 0, 2)).astype(jnp.bfloat16)


def kernel(
    offs_hbm, q_hbm, g_hbm, k_hbm, v_hbm, gq_hbm, recv_kv,
    offs, q_in, g_in, k_ref, v_ref, kt_ref,
    send_a, recv_a, send_q, recv_q, send_kv, gq_out,
    s_ref, dp_ref, pb_ref, gk_acc, gv_acc,
    in_sem, send_sem, recv_a_sem, recv_q_sem, recv_kv_sem, out_sem,
):
    devices = send_a.shape[0]
    toks = q_in.shape[0]
    half = toks // 2
    key_len, hd = k_ref.shape
    tile = 256
    tiles = key_len // tile
    rows = GROUP * toks
    scale = hd ** -0.5

    me = lax.axis_index("seq")
    slots = devices // GROUP
    ring = devices // 4
    my_y, my_z, my_c = me // (2 * ring), (me // 2) % ring, me % 2

    def partner(slot, j, m, sign):
        k = (slot % 2) * (GROUP // 4) + j
        dz = ring // 2 + k if m < 2 else ring // 2 - 1 - k
        y = 1 - my_y if slot < 2 else my_y
        z = lax.rem(my_z + dz if sign > 0 else my_z + ring - dz, ring)
        c = 1 - my_c if m % 2 == 0 else my_c
        return (y * ring + z) * 2 + c

    def each(slot, sign, act):
        def four(j, carry):
            for m in range(4):
                act(partner(slot, j, m, sign), 4 * j + m)
            return carry

        last = GROUP // 4 - 1
        if slot < slots - 1:
            lax.fori_loop(0, last + 1, four, 0)
        else:
            lax.fori_loop(0, last, four, 0)
            for m in range(3):
                act(partner(slot, last, m, sign), 4 * last + m)

    barrier = pltpu.get_barrier_semaphore()
    for slot in range(slots):
        each(slot, 1, lambda dev, i: pl.semaphore_signal(
            barrier, inc=1, device_id={"seq": dev}, device_id_type=MESH
        ))

    loads = [
        pltpu.make_async_copy(src, dst, in_sem.at[i])
        for i, (src, dst) in enumerate(
            ((q_hbm, q_in), (g_hbm, g_in), (k_hbm, k_ref), (v_hbm, v_ref), (offs_hbm, offs))
        )
    ]
    for load in loads:
        load.start()
    loads[0].wait()
    loads[1].wait()

    def exchange(slot, sign, src, dst, s_sem, r_sem):
        def one(dev, i):
            pltpu.make_async_remote_copy(
                src_ref=src(dev, i), dst_ref=dst(i), send_sem=s_sem, recv_sem=r_sem,
                device_id={"seq": dev}, device_id_type=MESH,
            ).start()

        each(slot, sign, one)
        if slot == slots - 1:
            pltpu.make_async_copy(src(me, GROUP - 1), dst(GROUP - 1), r_sem).start()

    for i in range(slots):
        heads = pl.ds(i * GROUP, GROUP)
        send_a[heads, 0:toks, :] = swap(q_in[:, heads, :])
        send_a[heads, toks : 2 * toks, :] = swap(g_in[:, heads, :])
    pl.semaphore_wait(barrier, devices - 1)
    for slot in range(slots):
        exchange(
            slot, 1, lambda dev, i: send_a.at[dev], lambda i: recv_a.at[slot, i],
            send_sem.at[0], recv_a_sem.at[slot],
        )

    for load in loads[2:]:
        load.wait()
    for t in range(tiles):
        span = pl.ds(t * tile, tile)
        kt_ref[:, span] = jnp.transpose(k_ref[span, :].astype(jnp.float32)).astype(jnp.bfloat16)
    gk_acc[...] = jnp.zeros_like(gk_acc)
    gv_acc[...] = jnp.zeros_like(gv_acc)

    lane = lax.broadcasted_iota(jnp.int32, (1, rows), 1)
    sub = lax.broadcasted_iota(jnp.int32, (tile, rows), 0)
    in_tok = lane % toks
    number = lane // toks
    shift = jnp.where(in_tok >= half, offs[2], offs[1]) - offs[0]
    local_pos = shift + in_tok % half

    def return_queries(step, gq_t):
        gq = jnp.transpose(gq_t * scale).astype(jnp.bfloat16)
        send_q[step] = gq.reshape(GROUP, toks, hd)
        exchange(
            step, -1, lambda dev, i: send_q.at[step, i], lambda i: recv_q.at[me],
            send_sem.at[1], recv_q_sem,
        )

    for step in range(slots):
        pltpu.make_async_copy(recv_a.at[step], recv_a.at[step], recv_a_sem.at[step]).wait()
        q = recv_a[step, :, 0:toks, :].reshape(rows, hd)
        g = recv_a[step, :, toks : 2 * toks, :].reshape(rows, hd)
        device = jnp.zeros_like(lane)
        for m in range(4):
            device = jnp.where(number % 4 == m, partner(step, number // 4, m, -1), device)
        limit = local_pos + half * device
        top = jnp.full((1, rows), -jnp.inf, jnp.float32)
        for t in range(tiles):
            span = pl.ds(t * tile, tile)
            s = nt_dot(k_ref[span, :], q)
            s = jnp.where(sub + t * tile <= limit, s, -jnp.inf)
            s_ref[span, :] = s
            top = jnp.maximum(top, jnp.max(s, axis=0, keepdims=True))
        total = jnp.zeros((1, rows), jnp.float32)
        for t in range(tiles):
            span = pl.ds(t * tile, tile)
            e = jnp.exp2((s_ref[span, :] - top) * (scale * math.log2(math.e)))
            s_ref[span, :] = e
            total = total + jnp.sum(e, axis=0, keepdims=True)
        inv = 1.0 / total
        delta = jnp.zeros((1, rows), jnp.float32)
        for t in range(tiles):
            span = pl.ds(t * tile, tile)
            p = s_ref[span, :] * inv
            pb = p.astype(jnp.bfloat16)
            dp = nt_dot(v_ref[span, :], g)
            s_ref[span, :] = p
            pb_ref[span, :] = pb
            dp_ref[span, :] = dp
            delta = delta + jnp.sum(pb.astype(jnp.float32) * dp, axis=0, keepdims=True)
        gq_t = jnp.zeros((hd, rows), jnp.float32)
        for t in range(tiles):
            span = pl.ds(t * tile, tile)
            ds = (s_ref[span, :] * (dp_ref[span, :] - delta)).astype(jnp.bfloat16)
            gq_t = gq_t + jnp.dot(kt_ref[:, span], ds, preferred_element_type=jnp.float32)
            gk_acc[span, :] += jnp.dot(ds, q, preferred_element_type=jnp.float32)
            gv_acc[span, :] += jnp.dot(pb_ref[span, :], g, preferred_element_type=jnp.float32)
        if step < slots - 1:
            return_queries(step, gq_t)

    for i in range(slots):
        span = pl.ds(i * rows, rows)
        owners = pl.ds(i * GROUP, GROUP)
        send_kv[owners, 0:toks, :] = (
            (gk_acc[span, :] * scale).astype(jnp.bfloat16).reshape(GROUP, toks, hd)
        )
        send_kv[owners, toks : 2 * toks, :] = (
            gv_acc[span, :].astype(jnp.bfloat16).reshape(GROUP, toks, hd)
        )
    for slot in range(slots):
        exchange(
            slot, 1, lambda dev, i: send_kv.at[dev], lambda i: recv_kv.at[me],
            send_sem.at[2], recv_kv_sem,
        )
        if slot == 1:
            return_queries(slots - 1, gq_t)

    stores = []

    def store(i, staged, out, heads):
        stores.append(
            pltpu.make_async_copy(staged.at[:, heads, :], out.at[:, heads, :], out_sem.at[i])
        )
        stores[-1].start()

    pltpu.make_async_copy(recv_q, recv_q, recv_q_sem).wait()
    for i in range(devices // GROUP):
        heads = pl.ds(i * GROUP, GROUP)
        gq_out[:, heads, :] = swap(recv_q[heads, :, :])
        store(i, gq_out, gq_hbm, heads)
    pltpu.make_async_copy(recv_kv, recv_kv, recv_kv_sem).wait()
    for copy in stores:
        copy.wait()
    for i, buf in enumerate((send_a, recv_q, send_kv)):
        sent = buf.at[pl.ds(0, devices - 1)]
        pltpu.make_async_copy(sent, sent, send_sem.at[i]).wait()


def by_token(gq_in, kv_in, gq_hbm, gk_hbm, gv_hbm, gq, kv, gk, gv, in_sem, out_sem):
    toks = gq.shape[0]
    slots = kv.shape[0] // GROUP
    groups = [pl.ds(i * GROUP, GROUP) for i in range(slots)]
    loads = [
        pltpu.make_async_copy(kv_in.at[heads], kv.at[heads], in_sem.at[i])
        for i, heads in enumerate(groups)
    ]
    loads.append(pltpu.make_async_copy(gq_in, gq, in_sem.at[slots]))
    for load in loads:
        load.start()
    stores = []

    def store(src, dst):
        stores.append(pltpu.make_async_copy(src, dst, out_sem.at[len(stores)]))
        stores[-1].start()

    for i, heads in enumerate(groups):
        loads[i].wait()
        gk[:, heads, :] = swap(kv[heads, 0:toks, :])
        store(gk.at[:, heads, :], gk_hbm.at[:, heads, :])
        gv[:, heads, :] = swap(kv[heads, toks : 2 * toks, :])
        store(gv.at[:, heads, :], gv_hbm.at[:, heads, :])
        if i == 0:
            loads[slots].wait()
            store(gq, gq_hbm)
    for copy in stores:
        copy.wait()


def body(queries, grad_out, keys, values, block_offsets):
    blocks, tok, heads, hd = queries.shape
    key_len = keys.shape[0]
    toks = blocks * tok
    rows = GROUP * toks
    bf16, f32 = jnp.bfloat16, jnp.float32
    hbm = pl.BlockSpec(memory_space=pl.ANY)
    out = jax.ShapeDtypeStruct((toks, heads, hd), bf16)
    gq, kv = pl.pallas_call(
        kernel,
        out_shape=(out, jax.ShapeDtypeStruct((heads, 2 * toks, hd), bf16)),
        in_specs=[hbm] * 5,
        out_specs=(hbm, hbm),
        scratch_shapes=[
            pltpu.SMEM((1 + blocks,), jnp.int32),
            pltpu.VMEM((toks, heads, hd), bf16),
            pltpu.VMEM((toks, heads, hd), bf16),
            pltpu.VMEM((key_len, hd), bf16),
            pltpu.VMEM((key_len, hd), bf16),
            pltpu.VMEM((hd, key_len), bf16),
            pltpu.VMEM((heads, 2 * toks, hd), bf16),
            pltpu.VMEM((heads // GROUP, GROUP, 2 * toks, hd), bf16),
            pltpu.VMEM((heads // GROUP, GROUP, toks, hd), bf16),
            pltpu.VMEM((heads, toks, hd), bf16),
            pltpu.VMEM((heads, 2 * toks, hd), bf16),
            pltpu.VMEM((toks, heads, hd), bf16),
            pltpu.VMEM((key_len, rows), f32),
            pltpu.VMEM((key_len, rows), f32),
            pltpu.VMEM((key_len, rows), bf16),
            pltpu.VMEM((key_len, hd), f32),
            pltpu.VMEM((key_len, hd), f32),
            pltpu.SemaphoreType.DMA((5,)),
            pltpu.SemaphoreType.DMA((3,)),
            pltpu.SemaphoreType.DMA((4,)),
            pltpu.SemaphoreType.DMA,
            pltpu.SemaphoreType.DMA,
            pltpu.SemaphoreType.DMA((4,)),
        ],
        compiler_params=pltpu.CompilerParams(
            collective_id=0, has_side_effects=True, vmem_limit_bytes=60 * MIB
        ),
        cost_estimate=pl.CostEstimate(
            flops=12 * blocks * tok * heads * key_len * hd,
            bytes_accessed=14 * toks * heads * hd,
            transcendentals=blocks * tok * heads * key_len,
        ),
        name="backward",
    )(
        block_offsets,
        queries.reshape(toks, heads, hd),
        grad_out.reshape(toks, heads, hd),
        keys.reshape(key_len, hd),
        values.reshape(key_len, hd),
    )
    gq, gk, gv = pl.pallas_call(
        by_token,
        out_shape=(out, out, out),
        in_specs=[hbm, hbm],
        out_specs=(hbm, hbm, hbm),
        scratch_shapes=[
            pltpu.VMEM((toks, heads, hd), bf16),
            pltpu.VMEM((heads, 2 * toks, hd), bf16),
            pltpu.VMEM((toks, heads, hd), bf16),
            pltpu.VMEM((toks, heads, hd), bf16),
            pltpu.SemaphoreType.DMA((1 + heads // GROUP,)),
            pltpu.SemaphoreType.DMA((1 + 2 * heads // GROUP,)),
        ],
        name="by_token",
    )(gq, kv)
    return gq.reshape(blocks, tok, heads, hd), gk, gv


def solution(mesh):
    in_specs = (
        P("batch", "seq", None, None),
        P("batch", "seq", None, None),
        P("batch", "seq", None),
        P("batch", "seq", None),
        P("batch"),
    )
    out_specs = (
        P("batch", "seq", None, None),
        P(("batch", "seq"), None, None),
        P(("batch", "seq"), None, None),
    )
    return jax.shard_map(body, mesh=mesh, in_specs=in_specs, out_specs=out_specs, check_vma=False)
```
